128 devices in a mesh: group: 16 (over z, y), member: 8 (over x, core).
Axes of the slice: x: 4, y: 4, z: 4, core: 2. Of those that a mesh axis runs over, the one named last changes fastest.
Arguments:
- tokens: bfloat16 [16384, 2048], P(('group', 'member')), may hold values from -6 to 6
- out_grad: bfloat16 [16384, 2048], P(('group', 'member')), may hold values from -6 to 6
- expert_ids: int32 [16384, 10], P(('group', 'member')), may hold values from 0 to 255, all different within a row; in each aligned block of 128 rows (0 to 127, 128 to 255, ...) at most 6 rows name the same one
- gate_vals: float32 [16384, 10], P(('group', 'member')), may hold values from 0.05 to 0.6
- w_gate: bfloat16 [256, 2048, 512], P(('group', 'member')), may hold values from -0.125 to 0.125
- w_up: bfloat16 [256, 2048, 512], P(('group', 'member')), may hold values from -0.125 to 0.125
- w_down: bfloat16 [256, 512, 2048], P(('group', 'member')), may hold values from -0.25 to 0.25
Outputs:
- grad_tokens: bfloat16 [16384, 2048], P(('group', 'member'))
- grad_w_gate: bfloat16 [256, 2048, 512], P(('group', 'member'))
- grad_w_up: bfloat16 [256, 2048, 512], P(('group', 'member'))
- grad_w_down: bfloat16 [256, 512, 2048], P(('group', 'member'))
The draws below stay inside these ranges and needn't reach their ends.
Inputs may be any that keep to these rules, and one draw needn't show every extreme that they name: `expert_ids`: each row names 10 different experts. Among the rows of one device no expert is named more than 6 times, a bound that some block reaches.
All inputs are finite; a program needn't handle non-finite values.
Results may differ from the reference program's by a relative error of at most 0.019.
Values may be sent and summed in bfloat16 or wider, within the bound.
A program may use at most 192 MiB of HBM per device.

```python
import math
import jax
import jax.numpy as jnp
import numpy as np
from jax import lax

D = 2048
H = 512
K = 10
TOK_DEV = 128
EXPERTS = 256
TOKENS = 16384
CAP = 6
N_GROUP = 16
N_MEMBER = 8


def steps_of(rng, shape, shards, least, top_value):
    def one(position, parts):
        steps = jax.random.uniform(jax.random.fold_in(jax.random.fold_in(rng, 6), position), (parts,), jnp.float32, least / len(shards), top_value / len(shards))
        return jnp.repeat(jnp.exp(steps), shape[position] // parts).reshape((-1,) + (1,) * (len(shape) - position - 1))

    loudness = one(*shards[0])
    for cut in shards[1:]:
        loudness = loudness * one(*cut)
    return loudness


def deal_out(own_key, own, number, rows, number_of, top, reach, lean):
    sequence = jax.random.permutation(own_key, number_of)
    heavy_load, common = shares(number_of, rows * top, reach, lean, True), shares(number_of, rows * top, reach, lean, False)
    places = jnp.arange(number_of)

    def named(sizes, offset_by):
        used = int((sizes > 0).sum())
        fixed = max(1, used // 4)
        moved = fixed + (places - fixed + offset_by * (used - fixed)) % max(1, number_of - fixed)
        return jnp.zeros((number_of,), jnp.int32).at[sequence[jnp.where(places < fixed, places, moved)]].set(jnp.asarray(sizes, jnp.int32))

    sizes = jnp.where(number % 4 == 0, named(heavy_load, number // 4), named(common, number - number // 4 - 1))
    mixed = jax.random.permutation(jax.random.fold_in(own, 3), number_of)
    source_of, sink = mixed[0:number_of // 2 * 2:2], mixed[1:number_of // 2 * 2:2]
    slack = jnp.minimum(sizes[source_of] - 1, reach - sizes[sink]) // 2
    slack = jnp.where((source_of == sequence[0]) | (sink == sequence[0]) | (sizes[sink] == 0), 0, jnp.maximum(slack, 0))
    moved = jax.random.randint(jax.random.fold_in(own, 4), (number_of // 2,), 0, 1 << 20) % (slack + 1)
    sizes = sizes.at[source_of].add(-moved).at[sink].add(moved)
    items = jnp.searchsorted(jnp.cumsum(sizes), jnp.arange(rows * top), side="right").astype(jnp.int32)
    listing = items.reshape(top, rows).T
    listing = listing[jax.random.permutation(jax.random.fold_in(own, 1), rows)]
    offset_by = jax.random.randint(jax.random.fold_in(own, 2), (rows, 1), 0, top)
    return jnp.take_along_axis(listing, (jnp.arange(top)[None, :] + offset_by) % top, axis=1)


def shares(number_of, total, bound, skew, full):
    weights = [(1 << 20) // math.isqrt(rank ** skew) + 1 for rank in range(1, number_of + 1)]
    largest = bound if full else min(bound, max(-(-total // number_of), total * weights[0] // sum(weights)))
    least = 1 if total - largest >= number_of - 1 else 0
    counts, surplus = [largest] + [least] * (number_of - 1), total - largest - least * (number_of - 1)
    while surplus > 0:
        free = [i for i in range(1, number_of) if counts[i] < largest] or [i for i in range(1, number_of) if counts[i] < bound]
        whole, remaining = sum([weights[i] for i in free]), surplus
        for i in free:
            more = min(bound - counts[i], max(1, remaining * weights[i] // whole), surplus)
            counts[i] = counts[i] + more
            surplus = surplus - more
    return np.array(counts)


def bell_draw(key, dims, spread, bound, split=(), held_as=jnp.bfloat16):
    values = jax.random.normal(key, dims, jnp.float32) * spread
    if len(split) > 0:
        values = steps_of(key, dims, split, -0.22, 0.18) * values
    return jnp.clip(values, min=-bound, max=bound).astype(held_as)


def setup_inputs(seed: int = 0) -> dict:
    arg_keys = jax.random.split(jax.random.key(seed), 8)
    tokens = bell_draw(arg_keys[0], (TOKENS, D), 1.0, 6.0, ((0, 128),))
    out_grad = bell_draw(arg_keys[1], (TOKENS, D), 1.0, 6.0, ((0, 128),))
    expert_ids_keys = jax.random.split(jax.random.fold_in(arg_keys[2], 1), TOKENS // TOK_DEV)
    expert_ids_turns = jax.random.permutation(jax.random.fold_in(arg_keys[2], 3), TOKENS // TOK_DEV)
    expert_ids = jax.vmap(lambda own, number: deal_out(jax.random.fold_in(arg_keys[2], 2), own, number, TOK_DEV, EXPERTS, K, CAP, 2))(expert_ids_keys, expert_ids_turns).reshape((TOKENS, K))
    gate_vals = jnp.clip(jnp.exp(math.log(0.6) - 2.4849067 * jax.random.uniform(arg_keys[3], (TOKENS, K), jnp.float32) ** steps_of(arg_keys[3], (TOKENS, K), ((0, 128),), -0.2, 0.2)), 0.05, 0.6)
    w_gate = bell_draw(arg_keys[4], (EXPERTS, D, H), D ** -0.5, 0.125, ((0, 128),))
    w_up = bell_draw(arg_keys[5], (EXPERTS, D, H), D ** -0.5, 0.125, ((0, 128),))
    w_down = bell_draw(arg_keys[6], (EXPERTS, H, D), H ** -0.5, 0.25, ((0, 128),))
    return dict(tokens=tokens, out_grad=out_grad, expert_ids=expert_ids, gate_vals=gate_vals, w_gate=w_gate, w_up=w_up, w_down=w_down)


def reference(tokens, out_grad, expert_ids, gate_vals, w_gate, w_up, w_down):
    devices = N_GROUP * N_MEMBER
    assigned = TOK_DEV * K
    slots_dev = EXPERTS * CAP
    ids = expert_ids.reshape(devices, assigned)
    experts_row = jnp.arange(EXPERTS).astype(jnp.int32)
    one_hot = (ids[:, :, None] == experts_row[None, None, :]).astype(jnp.int32)
    slot_rank = jnp.sum((jnp.cumsum(one_hot, axis=1) - one_hot) * one_hot, axis=2)
    slot_flat = ids * CAP + slot_rank
    device_row = jnp.arange(devices).astype(jnp.int32)[:, None]
    pair_row = jnp.arange(assigned).astype(jnp.int32)[None, :]
    token_global = device_row * TOK_DEV + pair_row // K
    where_flat = (device_row * slots_dev + slot_flat).reshape(-1)
    table = jnp.full((devices * slots_dev,), TOKENS, jnp.int32).at[where_flat].set(token_global.reshape(-1))
    gate_table = jnp.zeros((devices * slots_dev,), jnp.float32).at[where_flat].set(gate_vals.reshape(devices, assigned).reshape(-1))
    table = table.reshape(devices, EXPERTS, CAP).transpose(1, 0, 2).reshape(EXPERTS, devices * CAP)
    gate_table = gate_table.reshape(devices, EXPERTS, CAP).transpose(1, 0, 2).reshape(EXPERTS, devices * CAP)
    padded_x = jnp.concatenate([tokens, jnp.zeros((1, D), jnp.bfloat16)], axis=0)
    padded_dy = jnp.concatenate([out_grad, jnp.zeros((1, D), jnp.bfloat16)], axis=0)

    def per_expert(grad_acc, inputs):
        index_rows, gate_rows, gate_weight, up_weight, down_weight = inputs
        rows_x = padded_x[index_rows]
        rows_dy = padded_dy[index_rows]
        weight = gate_rows[:, None]
        pre_gate = jnp.dot(rows_x, gate_weight, preferred_element_type=jnp.float32)
        pre_up = jnp.dot(rows_x, up_weight, preferred_element_type=jnp.float32)
        sigmoid_gate = jax.nn.sigmoid(pre_gate)
        act_gate = pre_gate * sigmoid_gate
        hidden = act_gate * pre_up
        scaled = (weight * hidden).astype(jnp.bfloat16)
        grad_hidden = weight * jnp.dot(rows_dy, down_weight.T, preferred_element_type=jnp.float32)
        grad_pre_gate = (grad_hidden * pre_up * sigmoid_gate * (1.0 + pre_gate * (1.0 - sigmoid_gate))).astype(jnp.bfloat16)
        grad_pre_up = (grad_hidden * act_gate).astype(jnp.bfloat16)
        grad_down = jnp.dot(scaled.T, rows_dy, preferred_element_type=jnp.float32).astype(jnp.bfloat16)
        grad_gate = jnp.dot(rows_x.T, grad_pre_gate, preferred_element_type=jnp.float32).astype(jnp.bfloat16)
        grad_up = jnp.dot(rows_x.T, grad_pre_up, preferred_element_type=jnp.float32).astype(jnp.bfloat16)
        partial_value = jnp.dot(grad_pre_gate, gate_weight.T, preferred_element_type=jnp.float32)
        partial_value = partial_value + jnp.dot(grad_pre_up, up_weight.T, preferred_element_type=jnp.float32)
        grad_acc = grad_acc.at[index_rows].add(partial_value)
        return grad_acc, (grad_gate, grad_up, grad_down)

    start = jnp.zeros((TOKENS + 1, D), jnp.float32)
    grad_all, (grad_w_gate, grad_w_up, grad_w_down) = lax.scan(per_expert, start, (table, gate_table, w_gate, w_up, w_down))
    return grad_all[:TOKENS].astype(jnp.bfloat16), grad_w_gate, grad_w_up, grad_w_down
```

```python
import jax
import jax.numpy as jnp
from jax import lax
from jax.experimental import pallas as pl
from jax.experimental.pallas import tpu as pltpu
from jax.sharding import PartitionSpec as P

MESH = pl.DeviceIdType.MESH
BF = jnp.bfloat16
F32 = jnp.float32
PARTS = ((0, 768), (768, 640), (1408, 640))
AXES = ((0, 1, 2), (1, 2, 0), (2, 0, 1))
TOK = 128
CAP = 6
ROWS = 8 * CAP
HID = 512
TOPK = 10


def dot(a, b, contract):
    return lax.dot_general(a, b, ((contract[0], contract[1]), ((), ())), preferred_element_type=F32)


NN = ((1,), (0,))
NT = ((1,), (1,))
TN = ((0,), (0,))


def kernel(info, tok, dy, perm_in, wg, wu, wd, out_t, out_g, out_u, out_d, *rest):
    hold_dy, relay = rest[0:3], (rest[3:6], rest[6:9], rest[9:12])
    rest = rest[12:]
    near, send, got = rest[0:3], rest[3:6], (rest[6:9], rest[9:12])
    back, from_sib, last = rest[12:15], rest[15:18], rest[18:21]
    (ids, key, gate, pick, perm, tmp, act, pre, turned, wbuf, loc, ids_s, ids_r, ag_s, ag_r, d_s, d_r, b_s, b_r, z_s,
     z_r, w_sem, o_sem) = rest[21:]

    g = lax.axis_index("group")
    m = lax.axis_index("member")
    zyx = (g // 4, lax.rem(g, 4), m // 2)
    core = lax.rem(m, 2)

    def peer(axis, shift):
        pos = list(zyx)
        pos[axis] = lax.rem(pos[axis] + (shift + 4), 4)
        return (pos[0] * 4 + pos[1], pos[2] * 2 + core)

    sib = (g, zyx[2] * 2 + (1 - core))

    def remote(src, dst, ssem, rsem, to):
        return pltpu.make_async_remote_copy(
            src_ref=src, dst_ref=dst, send_sem=ssem, recv_sem=rsem, device_id=to, device_id_type=MESH
        )

    source = (tok, dy)
    gathered = (near, hold_dy)

    def cols(i):
        return pl.ds(PARTS[i][0], PARTS[i][1])

    def ids_line(i, u):
        return remote(info, ids.at[i, u, core], ids_s.at[i, u], ids_r.at[i, u], peer(AXES[i][0], u))

    def ids_own(i):
        return remote(info, ids.at[i, 0, core], ids_s.at[i, 0], ids_r.at[i, 0], sib)

    def ids_pass(i):
        part = ids.at[i, pl.ds(1, 3), core]
        return remote(part, part, ids_s.at[i, 4], ids_r.at[i, 4], sib)

    def ag_line(t, i, u):
        return remote(source[t].at[:, cols(i)], gathered[t][i].at[u, core], ag_s.at[t, i, u], ag_r.at[t, i, u],
                      peer(AXES[i][0], u))

    def ag_own(t, i):
        return remote(source[t].at[:, cols(i)], gathered[t][i].at[0, core], ag_s.at[t, i, 0], ag_r.at[t, i, 0], sib)

    def ag_pass(t, i, u):
        part = gathered[t][i].at[u, core]
        return remote(part, part, ag_s.at[t, i, 3 + u], ag_r.at[t, i, 3 + u], sib)

    def ag_self(t, i):
        return pltpu.make_async_copy(source[t].at[:, cols(i)], gathered[t][i].at[0, core], loc.at[t, i])

    def refill(i):
        return pltpu.make_async_copy(hold_dy[i], near[i], loc.at[2, i])

    def b0(t, i, e, r):
        k = r - 1
        return remote(send[i].at[e, r, 0], got[t][i].at[e, 0, r], d_s.at[t, i, e, k], d_r.at[t, i, e, k], peer(AXES[i][1], r))

    def b1(t, i, e, r):
        k = r + 2
        return remote(send[i].at[e, r, pl.ds(1, 3)], relay[t][i].at[e, :, r - 1], d_s.at[t, i, e, k], d_r.at[t, i, e, k],
                      peer(AXES[i][1], r))

    def c0(t, i, e, q):
        k = q + 5
        return remote(send[i].at[e, 0, q], got[t][i].at[e, q, 0], d_s.at[t, i, e, k], d_r.at[t, i, e, k], peer(AXES[i][2], q))

    def c1(t, i, e, q):
        k = q + 8
        return remote(relay[t][i].at[e, q - 1], got[t][i].at[e, q, pl.ds(1, 3)], d_s.at[t, i, e, k], d_r.at[t, i, e, k],
                      peer(AXES[i][2], q))

    def rc0(i, e, q):
        k = q - 1
        return remote(send[i].at[e, q, 0], back[i].at[e, 0, q], b_s.at[i, e, k], b_r.at[i, e, k], peer(AXES[i][2], -q))

    def rc1(i, e, q):
        k = q + 2
        return remote(send[i].at[e, q, pl.ds(1, 3)], relay[2][i].at[e, q - 1], b_s.at[i, e, k], b_r.at[i, e, k],
                      peer(AXES[i][2], -q))

    def rb0(i, e, r):
        k = r + 5
        return remote(send[i].at[e, 0, r], back[i].at[e, r, 0], b_s.at[i, e, k], b_r.at[i, e, k], peer(AXES[i][1], -r))

    def rb1(i, e, r):
        k = r + 8
        return remote(relay[2][i].at[e, :, r - 1], back[i].at[e, r, pl.ds(1, 3)], b_s.at[i, e, k], b_r.at[i, e, k],
                      peer(AXES[i][1], -r))

    def z_sib(i):
        return remote(near[i].at[:, 1 - core], from_sib[i], z_s.at[i, 0], z_r.at[i, 0], sib)

    def z_line(i, u):
        return remote(near[i].at[u, core], last[i].at[u - 1], z_s.at[i, u], z_r.at[i, u], peer(AXES[i][0], -u))

    weights = (wg, wu, wd)

    def load_w(n, e):
        return pltpu.make_async_copy(weights[n].at[e], wbuf[n], w_sem.at[n])

    outs = (out_g, out_u, out_d)

    def store_w(n, e):
        return pltpu.make_async_copy(wbuf[n], outs[n].at[e], o_sem.at[n])

    step = (1, 2, 3)

    barrier = pltpu.get_barrier_semaphore()
    for axis in range(3):
        for u in step:
            pl.semaphore_signal(barrier, inc=1, device_id=peer(axis, u), device_id_type=MESH)
    pl.semaphore_signal(barrier, inc=1, device_id=sib, device_id_type=MESH)
    for n in range(3):
        load_w(n, 0).start()
    load_p = pltpu.make_async_copy(perm_in, perm, loc.at[2, 3])
    load_p.start()
    for i in range(3):
        ag_self(0, i).start()
        ag_self(1, i).start()
        ids[i, 0, core] = info[...]
    pl.semaphore_wait(barrier, 10)

    for i in range(3):
        ids_own(i).start()
        for u in step:
            ids_line(i, u).start()
    for t in range(2):
        for u in step:
            for i in range(3):
                ag_line(t, i, u).start()
        for i in range(3):
            ag_own(t, i).start()
    for i in range(3):
        for u in step:
            ids_line(i, u).wait_recv()
        ids_pass(i).start()
    for i in range(3):
        ids_own(i).wait_recv()
        ids_pass(i).wait_recv()

    before = (lax.broadcasted_iota(jnp.int32, (TOK, TOK), 0) < lax.broadcasted_iota(jnp.int32, (TOK, TOK), 1))
    before = jnp.where(before, 1.0, 0.0).astype(BF)
    line = lax.broadcasted_iota(jnp.int32, (32, TOK), 0)
    for i in range(3):
        ax_a, ax_b, ax_c = AXES[i]
        shift = [0, 0, 0]
        shift[ax_b] = (line >> 2) & 3
        shift[ax_c] = line & 3
        at = [(zyx[n] + shift[n]) & 3 for n in range(3)]
        expert = ((((at[0] * 4 + at[1]) * 4 + at[2]) * 2 + core) * 2 + (line >> 4)).astype(F32)
        for u in range(4):
            for c in range(2):
                s = u * 2 + c
                named = jnp.zeros((32, TOK), F32)
                weight = jnp.zeros((32, TOK), F32)
                for k in range(TOPK):
                    same = ids[i, u, c, k:k + 1, :] == expert
                    named = named + jnp.where(same, 1.0, 0.0)
                    weight = weight + jnp.where(same, ids[i, u, c, TOPK + k:TOPK + k + 1, :], 0.0)
                rank = dot(named.astype(BF), before, NN)
                place = jnp.where(named > 0.5, rank + float(s * CAP), -1.0)
                for e in range(2):
                    key[i, e, :, s * TOK:(s + 1) * TOK] = place[e * 16:(e + 1) * 16]
                    gate[i, e, :, s * TOK:(s + 1) * TOK] = weight[e * 16:(e + 1) * 16]

    slot = lax.broadcasted_iota(jnp.int32, (ROWS, 8 * TOK), 0).astype(F32)

    def build_pick(i, e, weighted):
        def one(n, carry):
            same = key[i, e, pl.ds(n, 1), :] == slot
            value = gate[i, e, pl.ds(n, 1), :] if weighted else 1.0
            pick[n] = jnp.where(same, value, 0.0).astype(BF)
            return carry

        lax.fori_loop(0, 16, one, 0)

    def dispatch(t, i, e):
        width = PARTS[i][1]
        build_pick(i, e, t == 1)

        def half(h, carry):
            rows = pick[pl.ds(h * 8, 8)].reshape(8 * ROWS, 8 * TOK)
            value = dot(rows, near[i][...].reshape(8 * TOK, width), NN).astype(BF)
            send[i][e, pl.ds(2 * h, 2)] = value.reshape(2, 4, ROWS, width)
            return carry

        lax.fori_loop(0, 2, half, 0)
        got[t][i][e, 0, 0] = send[i][e, 0, 0]
        for r in step:
            b1(t, i, e, r).start()
        for r in step:
            c0(t, i, e, r).start()
        for r in step:
            b0(t, i, e, r).start()

    def forward(t, e):
        for i in range(3):
            for r in step:
                b1(t, i, e, r).wait_recv()
            for q in step:
                c1(t, i, e, q).start()

    def arrived(t, i, e):
        for r in step:
            b0(t, i, e, r).wait_recv()
            c0(t, i, e, r).wait_recv()
            c1(t, i, e, r).wait_recv()

    def sends_done(t, i, e):
        for r in step:
            b0(t, i, e, r).wait_send()
            b1(t, i, e, r).wait_send()
            c0(t, i, e, r).wait_send()

    def in_order(t, i, e):
        width = PARTS[i][1]

        def half(h, carry):
            rows = pl.ds(pl.multiple_of(h * 384, 384), 384)
            tmp[rows, :] = dot(perm[i - 1, rows, :], got[t][i][e].reshape(16 * ROWS, width), NN).astype(BF)
            return carry

        lax.fori_loop(0, 2, half, 0)
        got[t][i][e] = tmp[...].reshape(4, 4, ROWS, width)

    def each(count, body):
        lax.fori_loop(0, count, lambda n, c: (body(n), c)[1], 0)

    def gather_pass(t):
        for i in range(3):
            for u in step:
                ag_line(t, i, u).wait_recv()
                ag_pass(t, i, u).start()

    def gather_end(t, i):
        ag_own(t, i).wait_recv()
        for u in step:
            ag_pass(t, i, u).wait_recv()
            ag_pass(t, i, u).wait_send()
            ag_line(t, i, u).wait_send()
        ag_own(t, i).wait_send()
        ag_self(t, i).wait()

    gather_pass(0)
    for i in range(3):
        gather_end(0, i)
        each(2, lambda e: dispatch(0, i, e))
    gather_pass(1)
    each(2, lambda e: forward(0, e))

    for i in range(3):
        gather_end(1, i)
        refill(i).start()
    for i in range(3):
        refill(i).wait()

    def dispatch_dy(e):
        for i in range(3):
            sends_done(0, i, e)
            dispatch(1, i, e)

    each(2, dispatch_dy)

    load_p.wait()

    def halves(t, i, e, h):
        return got[t][i][e, pl.ds(2 * h, 2)].reshape(8 * ROWS, PARTS[i][1])

    def first(e):
        for i in range(3):
            arrived(0, i, e)
        for i in (1, 2):
            in_order(0, i, e)
        load_w(0, e).wait()
        load_w(1, e).wait()

        def half(h):
            for n in range(2):
                total = dot(halves(0, 0, e, h), wbuf[n][0:768], NN)
                for i in (1, 2):
                    total = total + dot(halves(0, i, e, h), wbuf[n][PARTS[i][0]:PARTS[i][0] + PARTS[i][1]], NN)
                pre[e, n, pl.ds(pl.multiple_of(h * 384, 384), 384)] = total

        each(2, half)
        load_w(0, 1 - e).start()
        load_w(1, 1 - e).start()
        forward(1, e)

    each(2, first)

    def second(e):
        for i in range(3):
            arrived(1, i, e)
        for i in (1, 2):
            in_order(1, i, e)
        for n in range(3):
            load_w(n, e).wait()

        def half(h):
            grad = dot(halves(1, 0, e, h), wbuf[2][:, 0:768], NT)
            for i in (1, 2):
                grad = grad + dot(halves(1, i, e, h), wbuf[2][:, PARTS[i][0]:PARTS[i][0] + PARTS[i][1]], NT)
            rows = pl.ds(pl.multiple_of(h * 384, 384), 384)
            pre_gate = pre[e, 0, rows]
            pre_up = pre[e, 1, rows]
            sig = jax.nn.sigmoid(pre_gate)
            silu = pre_gate * sig
            act[e, 0, rows] = (silu * pre_up).astype(BF)
            act[e, 1, rows] = (grad * pre_up * sig * (1.0 + pre_gate * (1.0 - sig))).astype(BF)
            act[e, 2, rows] = (grad * silu).astype(BF)

        each(2, half)
        for i in range(3):
            sends_done(1, i, e)
            start, width = PARTS[i]
            if i > 0:
                def turn(h):
                    rows = pl.ds(pl.multiple_of(h * 384, 384), 384)
                    for n in range(2):
                        turned[n, rows] = dot(perm[2 - i, rows, :], act[e, 1 + n], NN).astype(BF)

                each(2, turn)

            def part(h):
                rows = pl.ds(pl.multiple_of(h * 384, 384), 384)
                left = act[e, 1, rows] if i == 0 else turned[0, rows]
                right = act[e, 2, rows] if i == 0 else turned[1, rows]
                total = dot(left, wbuf[0][start:start + width], NT) + dot(right, wbuf[1][start:start + width], NT)
                send[i][e, pl.ds(2 * h, 2)] = total.astype(BF).reshape(2, 4, ROWS, width)

            each(2, part)
            back[i][e, 0, 0] = send[i][e, 0, 0]
            for q in step:
                rc1(i, e, q).start()
            for q in step:
                rb0(i, e, q).start()
            for q in step:
                rc0(i, e, q).start()

        @pl.when(e == 0)
        def _():
            for n in range(3):
                load_w(n, 1).start()

    each(2, second)

    def send_on(e):
        for i in range(3):
            for q in step:
                rc1(i, e, q).wait_recv()
            for r in step:
                rb1(i, e, r).start()

    def weight_grads(e):
        @pl.when(e == 1)
        def _():
            for n in range(3):
                store_w(n, 0).wait()

        for i in range(3):
            start, width = PARTS[i]
            rows_x = got[0][i][e].reshape(16 * ROWS, width)
            rows_dy = got[1][i][e].reshape(16 * ROWS, width)
            wbuf[0][start:start + width] = dot(rows_x, act[e, 1], TN).astype(BF)
            wbuf[1][start:start + width] = dot(rows_x, act[e, 2], TN).astype(BF)
            wbuf[2][:, start:start + width] = dot(act[e, 0], rows_dy, TN).astype(BF)
        for n in range(3):
            store_w(n, e).start()

    def collect(e):
        for i in range(3):
            width = PARTS[i][1]
            for r in step:
                rb0(i, e, r).wait_recv()
                rc0(i, e, r).wait_recv()
                rb1(i, e, r).wait_recv()
            build_pick(i, e, False)

            def block(u):
                rows = pick[:, :, pl.ds(pl.multiple_of(u * 256, 256), 256)].reshape(16 * ROWS, 256)
                total = dot(rows, back[i][e].reshape(16 * ROWS, width), TN).reshape(2, TOK, width)
                held = near[i][u].astype(F32)
                near[i][u] = jnp.where(e == 0, total, total + held).astype(BF)

            each(4, block)

            @pl.when(e == 1)
            def _():
                z_sib(i).start()

    def tail(e):
        send_on(e)
        weight_grads(e)

    each(2, tail)
    each(2, collect)

    for i in range(3):
        z_sib(i).wait_recv()
        z_sib(i).wait_send()
        for u in step:
            near[i][u, core] = (near[i][u, core].astype(F32) + from_sib[i][u].astype(F32)).astype(BF)
            z_line(i, u).start()
    for i in range(3):
        total = near[i][0, core].astype(F32) + from_sib[i][0].astype(F32)
        for u in step:
            z_line(i, u).wait_recv()
            total = total + last[i][u - 1].astype(F32)
        out_t[:, PARTS[i][0]:PARTS[i][0] + PARTS[i][1]] = total.astype(BF)

    for n in range(3):
        store_w(n, 1).wait()
    for i in range(3):
        for u in step:
            z_line(i, u).wait_send()
            ids_line(i, u).wait_send()
        ids_own(i).wait_send()
        ids_pass(i).wait_send()

    def drain(e):
        for i in range(3):
            for r in step:
                c1(0, i, e, r).wait_send()
                c1(1, i, e, r).wait_send()
                rc0(i, e, r).wait_send()
                rc1(i, e, r).wait_send()
                rb0(i, e, r).wait_send()
                rb1(i, e, r).wait_send()

    each(2, drain)


def per_device(tokens, out_grad, expert_ids, gate_vals, w_gate, w_up, w_down):
    width = tokens.shape[1]
    info = jnp.concatenate(
        [expert_ids.T.astype(F32), gate_vals.T, jnp.zeros((24 - 2 * TOPK, TOK), F32)], axis=0
    )
    row = jnp.arange(16 * ROWS)
    block, inner = row // 12, row % 12
    hi, mid, lo = block // 16, (block // 4) % 4, block % 4
    at = jnp.stack([(lo * 16 + hi * 4 + mid) * 12 + inner, (mid * 16 + lo * 4 + hi) * 12 + inner])
    perm = (at[:, :, None] == row[None, None, :]).astype(BF)

    any_ = pl.BlockSpec(memory_space=pl.ANY)
    vmem = pl.BlockSpec(memory_space=pltpu.VMEM)
    widths = [p[1] for p in PARTS]
    hbm_shapes = [jax.ShapeDtypeStruct((4, 2, TOK, c), BF) for c in widths]
    for _ in range(3):
        hbm_shapes += [jax.ShapeDtypeStruct((2, 3, 3, ROWS, c), BF) for c in widths]
    scratch = [pltpu.VMEM((4, 2, TOK, c), BF) for c in widths]
    for _ in range(4):
        scratch += [pltpu.VMEM((2, 4, 4, ROWS, c), BF) for c in widths]
    scratch += [pltpu.VMEM((4, TOK, c), BF) for c in widths]
    scratch += [pltpu.VMEM((3, TOK, c), BF) for c in widths]
    dma = pltpu.SemaphoreType.DMA
    scratch += [
        pltpu.VMEM((3, 4, 2, 24, TOK), F32),
        pltpu.VMEM((3, 2, 16, 8 * TOK), F32),
        pltpu.VMEM((3, 2, 16, 8 * TOK), F32),
        pltpu.VMEM((16, ROWS, 8 * TOK), BF),
        pltpu.VMEM((2, 16 * ROWS, 16 * ROWS), BF),
        pltpu.VMEM((16 * ROWS, 640), BF),
        pltpu.VMEM((2, 3, 16 * ROWS, HID), BF),
        pltpu.VMEM((2, 2, 16 * ROWS, HID), F32),
        pltpu.VMEM((2, 16 * ROWS, HID), BF),
        (pltpu.VMEM((width, HID), BF), pltpu.VMEM((width, HID), BF), pltpu.VMEM((HID, width), BF)),
        dma((3, 4)),
        dma((3, 5)), dma((3, 5)),
        dma((2, 3, 7)), dma((2, 3, 7)),
        dma((2, 3, 2, 12)), dma((2, 3, 2, 12)),
        dma((3, 2, 12)), dma((3, 2, 12)),
        dma((3, 4)), dma((3, 4)),
        dma((3,)), dma((3,)),
    ]
    results = pl.pallas_call(
        kernel,
        out_shape=[
            jax.ShapeDtypeStruct(tokens.shape, BF),
            jax.ShapeDtypeStruct(w_gate.shape, BF),
            jax.ShapeDtypeStruct(w_up.shape, BF),
            jax.ShapeDtypeStruct(w_down.shape, BF),
        ] + hbm_shapes,
        in_specs=[vmem] + [any_] * 6,
        out_specs=[vmem] + [any_] * (3 + len(hbm_shapes)),
        scratch_shapes=scratch,
        compiler_params=pltpu.CompilerParams(collective_id=0, has_side_effects=True, vmem_limit_bytes=63 * 10**6),
        cost_estimate=pl.CostEstimate(flops=60 * 10**9, bytes_accessed=60 * 10**6, transcendentals=10**6),
    )(info, tokens, out_grad, perm, w_gate, w_up, w_down)
    return tuple(results[:4])


def solution(mesh):
    rows = P(("group", "member"), None)
    whole = P(("group", "member"), None, None)
    return jax.shard_map(
        per_device,
        mesh=mesh,
        in_specs=(rows, rows, rows, rows, whole, whole, whole),
        out_specs=(rows, whole, whole, whole),
        check_vma=False,
    )
```

```python
import jax
import jax.numpy as jnp
from jax import lax
from jax.experimental import pallas as pl
from jax.experimental.pallas import tpu as pltpu
from jax.sharding import PartitionSpec as P

MESH = pl.DeviceIdType.MESH
BF = jnp.bfloat16
F32 = jnp.float32
PARTS = ((0, 768), (768, 640), (1408, 640))
AXES = ((0, 1, 2), (1, 2, 0), (2, 0, 1))
TOK = 128
CAP = 6
ROWS = 8 * CAP
HID = 512
TOPK = 10


def dot(a, b, contract):
    return lax.dot_general(a, b, ((contract[0], contract[1]), ((), ())), preferred_element_type=F32)


NN = ((1,), (0,))
NT = ((1,), (1,))
TN = ((0,), (0,))


def kernel(ids_in, gates_in, tok, dy, wg, wu, wd, out_t, out_g, out_u, out_d, *rest):
    hold_dy, relay = rest[0:3], (rest[3:6], rest[6:9], rest[9:12])
    rest = rest[12:]
    near, send, got = rest[0:3], rest[3:6], (rest[6:9], rest[9:12])
    back, from_sib, last = rest[12:15], rest[15:18], rest[18:21]
    (info, ids, key, gate, pick, perm, tmp, act, pre, turned, wbuf, loc, ids_s, ids_r, ag_s, ag_r, d_s, d_r, b_s, b_r, z_s,
     z_r, w_sem, o_sem) = rest[21:]

    g = lax.axis_index("group")
    m = lax.axis_index("member")
    zyx = (g // 4, lax.rem(g, 4), m // 2)
    core = lax.rem(m, 2)

    def peer(axis, shift):
        pos = list(zyx)
        pos[axis] = lax.rem(pos[axis] + (shift + 4), 4)
        return (pos[0] * 4 + pos[1], pos[2] * 2 + core)

    sib = (g, zyx[2] * 2 + (1 - core))

    def remote(src, dst, ssem, rsem, to):
        return pltpu.make_async_remote_copy(
            src_ref=src, dst_ref=dst, send_sem=ssem, recv_sem=rsem, device_id=to, device_id_type=MESH
        )

    source = (tok, dy)
    gathered = (near, hold_dy)

    def cols(i):
        return pl.ds(PARTS[i][0], PARTS[i][1])

    def ids_line(i, u):
        return remote(info, ids.at[i, u, core], ids_s.at[i, u], ids_r.at[i, u], peer(AXES[i][0], u))

    def ids_own(i):
        return remote(info, ids.at[i, 0, core], ids_s.at[i, 0], ids_r.at[i, 0], sib)

    def ids_pass(i):
        part = ids.at[i, pl.ds(1, 3), core]
        return remote(part, part, ids_s.at[i, 4], ids_r.at[i, 4], sib)

    def ag_line(t, i, u):
        return remote(source[t].at[:, cols(i)], gathered[t][i].at[u, core], ag_s.at[t, i, u], ag_r.at[t, i, u],
                      peer(AXES[i][0], u))

    def ag_own(t, i):
        return remote(source[t].at[:, cols(i)], gathered[t][i].at[0, core], ag_s.at[t, i, 0], ag_r.at[t, i, 0], sib)

    def ag_pass(t, i, u):
        part = gathered[t][i].at[u, core]
        return remote(part, part, ag_s.at[t, i, 3 + u], ag_r.at[t, i, 3 + u], sib)

    def ag_self(i):
        return pltpu.make_async_copy(tok.at[:, cols(i)], near[i].at[0, core], loc.at[0, i])

    def refill(i):
        far, own = pl.ds(1, 3), 1 - core
        return (
            pltpu.make_async_copy(hold_dy[i].at[far], near[i].at[far], loc.at[1, i]),
            pltpu.make_async_copy(hold_dy[i].at[0, own], near[i].at[0, own], loc.at[2, i]),
            pltpu.make_async_copy(dy.at[:, cols(i)], near[i].at[0, core], loc.at[3, i]),
        )

    def b0(t, i, e, r):
        k = r - 1
        return remote(send[i].at[e, r, 0], got[t][i].at[e, 0, r], d_s.at[t, i, e, k], d_r.at[t, i, e, k], peer(AXES[i][1], r))

    def b1(t, i, e, r):
        k = r + 2
        return remote(send[i].at[e, r, pl.ds(1, 3)], relay[t][i].at[e, :, r - 1], d_s.at[t, i, e, k], d_r.at[t, i, e, k],
                      peer(AXES[i][1], r))

    def c0(t, i, e, q):
        k = q + 5
        return remote(send[i].at[e, 0, q], got[t][i].at[e, q, 0], d_s.at[t, i, e, k], d_r.at[t, i, e, k], peer(AXES[i][2], q))

    def c1(t, i, e, q):
        k = q + 8
        return remote(relay[t][i].at[e, q - 1], got[t][i].at[e, q, pl.ds(1, 3)], d_s.at[t, i, e, k], d_r.at[t, i, e, k],
                      peer(AXES[i][2], q))

    def rc0(i, e, q):
        k = q - 1
        return remote(send[i].at[e, q, 0], back[i].at[e, 0, q], b_s.at[i, e, k], b_r.at[i, e, k], peer(AXES[i][2], -q))

    def rc1(i, e, q):
        k = q + 2
        return remote(send[i].at[e, q, pl.ds(1, 3)], relay[2][i].at[e, q - 1], b_s.at[i, e, k], b_r.at[i, e, k],
                      peer(AXES[i][2], -q))

    def rb0(i, e, r):
        k = r + 5
        return remote(send[i].at[e, 0, r], back[i].at[e, r, 0], b_s.at[i, e, k], b_r.at[i, e, k], peer(AXES[i][1], -r))

    def rb1(i, e, r):
        k = r + 8
        return remote(relay[2][i].at[e, :, r - 1], back[i].at[e, r, pl.ds(1, 3)], b_s.at[i, e, k], b_r.at[i, e, k],
                      peer(AXES[i][1], -r))

    def z_sib(i, u):
        return remote(near[i].at[u, 1 - core], from_sib[i].at[u], z_s.at[i, u], z_r.at[i, u], sib)

    def z_line(i, u):
        return remote(near[i].at[u, core], last[i].at[u - 1], z_s.at[i, 3 + u], z_r.at[i, 3 + u], peer(AXES[i][0], -u))

    weights = (wg, wu, wd)

    def load_w(n, e):
        return pltpu.make_async_copy(weights[n].at[e], wbuf[n], w_sem.at[n])

    outs = (out_g, out_u, out_d)

    def store_w(n, e):
        return pltpu.make_async_copy(wbuf[n], outs[n].at[e], o_sem.at[n])

    step = (1, 2, 3)

    barrier = pltpu.get_barrier_semaphore()
    for axis in range(3):
        for u in step:
            pl.semaphore_signal(barrier, inc=1, device_id=peer(axis, u), device_id_type=MESH)
    pl.semaphore_signal(barrier, inc=1, device_id=sib, device_id_type=MESH)
    for n in range(3):
        load_w(n, 0).start()
    info[...] = jnp.zeros((32, TOK), F32)
    info[0:TOPK] = ids_in[...].astype(F32)
    info[16:16 + TOPK] = gates_in[...]
    for i in range(3):
        ag_self(i).start()
        ids[i, 0, core] = info[...]
    pl.semaphore_wait(barrier, 10)

    for i in range(3):
        ids_own(i).start()
        for u in step:
            ids_line(i, u).start()

    def gather_start(t):
        for u in (1, 3, 2):
            for i in range(3):
                ag_line(t, i, u).start()
        for i in range(3):
            ag_own(t, i).start()

    def gather_pass(t):
        for u in (1, 3, 2):
            for i in range(3):
                ag_line(t, i, u).wait_recv()
                ag_pass(t, i, u).start()

    def gather_end(t, i):
        ag_own(t, i).wait_recv()
        for u in (1, 2, 3):
            ag_pass(t, i, u).wait_recv()
            ag_pass(t, i, u).wait_send()
            ag_line(t, i, u).wait_send()
        ag_own(t, i).wait_send()

    gather_start(0)
    gather_start(1)
    for i in range(3):
        for u in step:
            ids_line(i, u).wait_recv()
        ids_pass(i).start()

    def build_perm(n, carry):
        row = lax.broadcasted_iota(jnp.int32, (192, TOK), 0) + n * 192
        group = (row * 5462) >> 16
        inner = row - group * 12
        hi, mid, lo = group >> 4, (group >> 2) & 3, group & 3
        rows = pl.ds(pl.multiple_of(n * 192, 192), 192)
        lane = lax.broadcasted_iota(jnp.int32, (192, TOK), 1)
        for way, target in enumerate((lo * 16 + hi * 4 + mid, mid * 16 + lo * 4 + hi)):
            ahead = target * 12 + inner - lane
            for c in range(6):
                perm[way, rows, c * TOK:(c + 1) * TOK] = jnp.where(ahead == c * TOK, 1.0, 0.0).astype(BF)
        return carry

    lax.fori_loop(0, 4, build_perm, 0)
    for i in range(3):
        ids_own(i).wait_recv()
        ids_pass(i).wait_recv()

    before = (lax.broadcasted_iota(jnp.int32, (TOK, TOK), 0) < lax.broadcasted_iota(jnp.int32, (TOK, TOK), 1))
    before = jnp.where(before, 1.0, 0.0).astype(BF)
    line = lax.broadcasted_iota(jnp.int32, (32, TOK), 0)
    for i in range(3):
        ax_a, ax_b, ax_c = AXES[i]
        shift = [0, 0, 0]
        shift[ax_b] = (line >> 2) & 3
        shift[ax_c] = line & 3
        at = [(zyx[n] + shift[n]) & 3 for n in range(3)]
        expert = ((((at[0] * 4 + at[1]) * 4 + at[2]) * 2 + core) * 2 + (line >> 4)).astype(F32)
        for u in range(4):
            for c in range(2):
                s = u * 2 + c
                named = jnp.zeros((32, TOK), F32)
                weight = jnp.zeros((32, TOK), F32)
                for k in range(TOPK):
                    same = ids[i, u, c, k:k + 1, :] == expert
                    named = named + jnp.where(same, 1.0, 0.0)
                    weight = weight + jnp.where(same, ids[i, u, c, 16 + k:17 + k, :], 0.0)
                rank = dot(named.astype(BF), before, NN)
                place = jnp.where(named > 0.5, rank + float(s * CAP), -1.0)
                for e in range(2):
                    key[i, e, :, s * TOK:(s + 1) * TOK] = place[e * 16:(e + 1) * 16]
                    gate[i, e, :, s * TOK:(s + 1) * TOK] = weight[e * 16:(e + 1) * 16]

    slot = lax.broadcasted_iota(jnp.int32, (ROWS, 8 * TOK), 0).astype(F32)

    def build_pick(i, e, weighted, keep=False):
        def one(n, carry):
            same = key[i, e, pl.ds(n, 1), :] == slot
            value = gate[i, e, pl.ds(n, 1), :] if weighted else 1.0
            picked = jnp.where(same, value, 0.0).astype(BF)
            if keep:
                for half in range(2):
                    got[1][i][half, n // 4, lax.rem(n, 4), :, 0:512] = picked[:, half * 512:half * 512 + 512]
            else:
                pick[n] = picked
            return carry

        lax.fori_loop(0, 16, one, 0)

    def dispatch(t, i, e):
        width = PARTS[i][1]
        build_pick(i, e, t == 1)

        def half(h, carry):
            rows = pick[pl.ds(h * 8, 8)].reshape(8 * ROWS, 8 * TOK)
            value = dot(rows, near[i][...].reshape(8 * TOK, width), NN).astype(BF)
            send[i][e, pl.ds(2 * h, 2)] = value.reshape(2, 4, ROWS, width)
            return carry

        lax.fori_loop(0, 2, half, 0)
        got[t][i][e, 0, 0] = send[i][e, 0, 0]
        for r in step:
            b1(t, i, e, r).start()
        for r in step:
            c0(t, i, e, r).start()
        for r in step:
            b0(t, i, e, r).start()

    def forward(t, e):
        for i in range(3):
            for r in step:
                b1(t, i, e, r).wait_recv()
        for q in (1, 3, 2):
            for i in range(3):
                c1(t, i, e, q).start()

    def arrived(t, i, e):
        for r in step:
            b0(t, i, e, r).wait_recv()
            c0(t, i, e, r).wait_recv()
            c1(t, i, e, r).wait_recv()

    def sends_done(t, i, e):
        for r in step:
            b0(t, i, e, r).wait_send()
            b1(t, i, e, r).wait_send()
            c0(t, i, e, r).wait_send()

    def in_order(t, i, e):
        width = PARTS[i][1]

        def half(h, carry):
            rows = pl.ds(pl.multiple_of(h * 384, 384), 384)
            tmp[rows, :] = dot(perm[i - 1, rows, :], got[t][i][e].reshape(16 * ROWS, width), NN).astype(BF)
            return carry

        lax.fori_loop(0, 2, half, 0)
        got[t][i][e] = tmp[...].reshape(4, 4, ROWS, width)

    def each(count, body):
        lax.fori_loop(0, count, lambda n, c: (body(n), c)[1], 0)

    gather_pass(0)
    for i in range(3):
        gather_end(0, i)
        ag_self(i).wait()

    def dispatch_tok(e):
        for i in range(3):
            dispatch(0, i, e)

    each(2, dispatch_tok)
    gather_pass(1)
    each(2, lambda e: forward(0, e))

    for i in range(3):
        gather_end(1, i)
        for one in refill(i):
            one.start()
    for i in range(3):
        for one in refill(i):
            one.wait()

    def dispatch_dy(e):
        for i in range(3):
            sends_done(0, i, e)
            dispatch(1, i, e)

    each(2, dispatch_dy)

    def halves(t, i, e, h):
        return got[t][i][e, pl.ds(2 * h, 2)].reshape(8 * ROWS, PARTS[i][1])

    def first(e):
        for i in range(3):
            arrived(0, i, e)
        for i in (1, 2):
            in_order(0, i, e)
        load_w(0, e).wait()
        load_w(1, e).wait()

        def half(h):
            both = []
            for n in range(2):
                total = dot(halves(0, 0, e, h), wbuf[n][0:768], NN)
                for i in (1, 2):
                    total = total + dot(halves(0, i, e, h), wbuf[n][PARTS[i][0]:PARTS[i][0] + PARTS[i][1]], NN)
                both.append(total)
            pre_gate, pre_up = both
            rows = pl.ds(pl.multiple_of(h * 384, 384), 384)
            sig = jax.nn.sigmoid(pre_gate)
            silu = pre_gate * sig
            act[e, 0, rows] = (silu * pre_up).astype(BF)
            pre[e, 0, rows] = pre_up * sig * (1.0 + pre_gate * (1.0 - sig))
            pre[e, 1, rows] = silu

        each(2, half)
        load_w(0, 1 - e).start()
        load_w(1, 1 - e).start()
        forward(1, e)

    each(2, first)

    def second(e):
        for i in range(3):
            arrived(1, i, e)
        for i in (1, 2):
            in_order(1, i, e)
        for n in range(3):
            load_w(n, e).wait()

        def half(h):
            grad = dot(halves(1, 0, e, h), wbuf[2][:, 0:768], NT)
            for i in (1, 2):
                grad = grad + dot(halves(1, i, e, h), wbuf[2][:, PARTS[i][0]:PARTS[i][0] + PARTS[i][1]], NT)
            rows = pl.ds(pl.multiple_of(h * 384, 384), 384)
            act[e, 1, rows] = (grad * pre[e, 0, rows]).astype(BF)
            act[e, 2, rows] = (grad * pre[e, 1, rows]).astype(BF)

        each(2, half)
        for i in range(3):
            sends_done(1, i, e)
            start, width = PARTS[i]
            if i > 0:
                def turn(h):
                    rows = pl.ds(pl.multiple_of(h * 384, 384), 384)
                    for n in range(2):
                        turned[n, rows] = dot(perm[2 - i, rows, :], act[e, 1 + n], NN).astype(BF)

                each(2, turn)

            def part(h):
                rows = pl.ds(pl.multiple_of(h * 384, 384), 384)
                left = act[e, 1, rows] if i == 0 else turned[0, rows]
                right = act[e, 2, rows] if i == 0 else turned[1, rows]
                total = dot(left, wbuf[0][start:start + width], NT) + dot(right, wbuf[1][start:start + width], NT)
                send[i][e, pl.ds(2 * h, 2)] = total.astype(BF).reshape(2, 4, ROWS, width)

            each(2, part)
            back[i][e, 0, 0] = send[i][e, 0, 0]
            for q in step:
                rc1(i, e, q).start()
            for q in step:
                rb0(i, e, q).start()
            for q in step:
                rc0(i, e, q).start()

        @pl.when(e == 0)
        def _():
            for n in range(3):
                load_w(n, 1).start()

    each(2, second)

    def send_on(e):
        for i in range(3):
            for q in step:
                rc1(i, e, q).wait_recv()
        for r in (1, 3, 2):
            for i in range(3):
                rb1(i, e, r).start()

    def weight_grads(e):
        @pl.when(e == 1)
        def _():
            for n in range(3):
                store_w(n, 0).wait()

        for i in range(3):
            start, width = PARTS[i]
            rows_x = got[0][i][e].reshape(16 * ROWS, width)
            rows_dy = got[1][i][e].reshape(16 * ROWS, width)
            wbuf[0][start:start + width] = dot(rows_x, act[e, 1], TN).astype(BF)
            wbuf[1][start:start + width] = dot(rows_x, act[e, 2], TN).astype(BF)
            wbuf[2][:, start:start + width] = dot(act[e, 0], rows_dy, TN).astype(BF)
        for n in range(3):
            store_w(n, e).start()

    def returned(i, e):
        for r in step:
            rb0(i, e, r).wait_recv()
            rc0(i, e, r).wait_recv()
            rb1(i, e, r).wait_recv()

    def collect(i):
        width = PARTS[i][1]
        build_pick(i, 0, False)
        returned(i, 0)
        for u in range(4):
            rows = pick[:, :, u * 256:(u + 1) * 256].reshape(16 * ROWS, 256)
            total = dot(rows, back[i][0].reshape(16 * ROWS, width), TN).reshape(2, TOK, width)
            near[i][u] = total.astype(BF)

    def collect_last(i, u):
        width = PARTS[i][1]
        lanes = (u % 2) * 256
        rows = got[1][i][u // 2, :, :, :, lanes:lanes + 256].reshape(16 * ROWS, 256)
        total = dot(rows, back[i][1].reshape(16 * ROWS, width), TN).reshape(2, TOK, width)
        near[i][u] = (total + near[i][u].astype(F32)).astype(BF)
        z_sib(i, u).start()

    def both(i, u):
        z_sib(i, u).wait_recv()
        return near[i][u, core].astype(F32) + from_sib[i][u].astype(F32)

    def line_out(i, u):
        near[i][u, core] = both(i, u).astype(BF)
        z_line(i, u).start()

    def tail(e):
        send_on(e)
        weight_grads(e)

    each(2, tail)
    for i in range(3):
        collect(i)
    for i in range(3):
        build_pick(i, 1, False, True)
    for i in range(3):
        returned(i, 1)
        collect_last(i, 2)
    for n, u in enumerate((1, 3, 0)):
        for i in range(3):
            collect_last(i, u)
        for i in range(3):
            line_out(i, (2, 1, 3)[n])
    for i in range(3):
        total = both(i, 0)
        for u in step:
            z_line(i, u).wait_recv()
            total = total + last[i][u - 1].astype(F32)
        out_t[:, PARTS[i][0]:PARTS[i][0] + PARTS[i][1]] = total.astype(BF)

    for n in range(3):
        store_w(n, 1).wait()
    for i in range(3):
        for u in range(4):
            z_sib(i, u).wait_send()
        for u in step:
            z_line(i, u).wait_send()
            ids_line(i, u).wait_send()
        ids_own(i).wait_send()
        ids_pass(i).wait_send()

    def drain(e):
        for i in range(3):
            for r in step:
                c1(0, i, e, r).wait_send()
                c1(1, i, e, r).wait_send()
                rc0(i, e, r).wait_send()
                rc1(i, e, r).wait_send()
                rb0(i, e, r).wait_send()
                rb1(i, e, r).wait_send()

    each(2, drain)


def copy_kernel(*refs):
    src, dst, held, sems = refs[:4], refs[4:8], refs[8:12], refs[12]
    moves = [(0, (pl.ds(0, TOK),))]
    for k in range(8):
        for n in (1, 2, 3):
            size = src[n].shape[1] // 4
            moves.append((n, (k // 4, pl.ds((k % 4) * size, size))))
    into = [pltpu.make_async_copy(src[n].at[at], held[n].at[at], sems.at[0, j]) for j, (n, at) in enumerate(moves)]
    out = [pltpu.make_async_copy(held[n].at[at], dst[n].at[at], sems.at[1, j]) for j, (n, at) in enumerate(moves)]
    for one in into:
        one.start()
    for one, other in zip(into, out):
        one.wait()
        other.start()
    for one in out:
        one.wait()


def hand_over(*arrays):
    any_ = pl.BlockSpec(memory_space=pl.ANY)
    return pl.pallas_call(
        copy_kernel,
        out_shape=[jax.ShapeDtypeStruct(a.shape, a.dtype) for a in arrays],
        in_specs=[any_] * 4,
        out_specs=[any_] * 4,
        scratch_shapes=[pltpu.VMEM(a.shape, a.dtype) for a in arrays] + [pltpu.SemaphoreType.DMA((2, 25))],
        compiler_params=pltpu.CompilerParams(vmem_limit_bytes=63 * 10**6),
        cost_estimate=pl.CostEstimate(flops=0, bytes_accessed=26 * 10**6, transcendentals=0),
    )(*arrays)


def per_device(tokens, out_grad, expert_ids, gate_vals, w_gate, w_up, w_down):
    width = tokens.shape[1]
    any_ = pl.BlockSpec(memory_space=pl.ANY)
    vmem = pl.BlockSpec(memory_space=pltpu.VMEM)
    widths = [p[1] for p in PARTS]
    hbm_shapes = [jax.ShapeDtypeStruct((4, 2, TOK, c), BF) for c in widths]
    for _ in range(3):
        hbm_shapes += [jax.ShapeDtypeStruct((2, 3, 3, ROWS, c), BF) for c in widths]
    scratch = [pltpu.VMEM((4, 2, TOK, c), BF) for c in widths]
    for _ in range(4):
        scratch += [pltpu.VMEM((2, 4, 4, ROWS, c), BF) for c in widths]
    scratch += [pltpu.VMEM((4, TOK, c), BF) for c in widths]
    scratch += [pltpu.VMEM((3, TOK, c), BF) for c in widths]
    dma = pltpu.SemaphoreType.DMA
    scratch += [
        pltpu.VMEM((32, TOK), F32),
        pltpu.VMEM((3, 4, 2, 32, TOK), F32),
        pltpu.VMEM((3, 2, 16, 8 * TOK), F32),
        pltpu.VMEM((3, 2, 16, 8 * TOK), F32),
        pltpu.VMEM((16, ROWS, 8 * TOK), BF),
        pltpu.VMEM((2, 16 * ROWS, 16 * ROWS), BF),
        pltpu.VMEM((16 * ROWS, 640), BF),
        pltpu.VMEM((2, 3, 16 * ROWS, HID), BF),
        pltpu.VMEM((2, 2, 16 * ROWS, HID), F32),
        pltpu.VMEM((2, 16 * ROWS, HID), BF),
        (pltpu.VMEM((width, HID), BF), pltpu.VMEM((width, HID), BF), pltpu.VMEM((HID, width), BF)),
        dma((4, 3)),
        dma((3, 5)), dma((3, 5)),
        dma((2, 3, 7)), dma((2, 3, 7)),
        dma((2, 3, 2, 12)), dma((2, 3, 2, 12)),
        dma((3, 2, 12)), dma((3, 2, 12)),
        dma((3, 7)), dma((3, 7)),
        dma((3,)), dma((3,)),
    ]
    results = pl.pallas_call(
        kernel,
        out_shape=[
            jax.ShapeDtypeStruct(tokens.shape, BF),
            jax.ShapeDtypeStruct(w_gate.shape, BF),
            jax.ShapeDtypeStruct(w_up.shape, BF),
            jax.ShapeDtypeStruct(w_down.shape, BF),
        ] + hbm_shapes,
        in_specs=[vmem, vmem] + [any_] * 5,
        out_specs=[vmem] + [any_] * (3 + len(hbm_shapes)),
        scratch_shapes=scratch,
        compiler_params=pltpu.CompilerParams(collective_id=0, has_side_effects=True, vmem_limit_bytes=63 * 10**6),
        cost_estimate=pl.CostEstimate(flops=60 * 10**9, bytes_accessed=60 * 10**6, transcendentals=10**6),
    )(expert_ids.T, gate_vals.T, tokens, out_grad, w_gate, w_up, w_down)
    return hand_over(*results[:4])


def solution(mesh):
    rows = P(("group", "member"), None)
    whole = P(("group", "member"), None, None)
    return jax.shard_map(
        per_device,
        mesh=mesh,
        in_specs=(rows, rows, rows, rows, whole, whole, whole),
        out_specs=(rows, whole, whole, whole),
        check_vma=False,
    )
```

```python
import jax
import jax.numpy as jnp
from jax import lax
from jax.experimental import pallas as pl
from jax.experimental.pallas import tpu as pltpu
from jax.sharding import PartitionSpec as P

MESH = pl.DeviceIdType.MESH
BF = jnp.bfloat16
F32 = jnp.float32
PARTS = ((0, 768), (768, 640), (1408, 640))
AXES = ((0, 1, 2), (1, 2, 0), (2, 0, 1))
TOK = 128
CAP = 6
ROWS = 8 * CAP
HID = 512
TOPK = 10


def dot(a, b, contract):
    return lax.dot_general(a, b, ((contract[0], contract[1]), ((), ())), preferred_element_type=F32)


NN = ((1,), (0,))
NT = ((1,), (1,))
TN = ((0,), (0,))


def kernel(ids_in, gates_in, tok, dy, wg, wu, wd, out_t, out_g, out_u, out_d, *rest):
    hold_dy, relay = rest[0:3], (rest[3:6], rest[6:9], rest[9:12])
    rest = rest[12:]
    near, send, got = rest[0:3], rest[3:6], (rest[6:9], rest[9:12])
    back, from_sib, last = rest[12:15], rest[15:18], rest[18:21]
    (info, ids, key, gate, pick, perm, tmp, act, pre, turned, wbuf, loc, ids_s, ids_r, ag_s, ag_r, d_s, d_r, b_s, b_r, z_s,
     z_r, w_sem, o_sem) = rest[21:]

    g = lax.axis_index("group")
    m = lax.axis_index("member")
    zyx = (g // 4, lax.rem(g, 4), m // 2)
    core = lax.rem(m, 2)

    def peer(axis, shift):
        pos = list(zyx)
        pos[axis] = lax.rem(pos[axis] + (shift + 4), 4)
        return (pos[0] * 4 + pos[1], pos[2] * 2 + core)

    sib = (g, zyx[2] * 2 + (1 - core))

    def remote(src, dst, ssem, rsem, to):
        return pltpu.make_async_remote_copy(
            src_ref=src, dst_ref=dst, send_sem=ssem, recv_sem=rsem, device_id=to, device_id_type=MESH
        )

    source = (tok, dy)
    gathered = (near, hold_dy)

    def cols(i):
        return pl.ds(PARTS[i][0], PARTS[i][1])

    def ids_line(i, u):
        return remote(info, ids.at[i, u, core], ids_s.at[i, u], ids_r.at[i, u], peer(AXES[i][0], u))

    def ids_own(i):
        return remote(info, ids.at[i, 0, core], ids_s.at[i, 0], ids_r.at[i, 0], sib)

    def ids_pass(i):
        part = ids.at[i, pl.ds(1, 3), core]
        return remote(part, part, ids_s.at[i, 4], ids_r.at[i, 4], sib)

    def ag_line(t, i, u):
        return remote(source[t].at[:, cols(i)], gathered[t][i].at[u, core], ag_s.at[t, i, u], ag_r.at[t, i, u],
                      peer(AXES[i][0], u))

    def ag_own(t, i):
        return remote(source[t].at[:, cols(i)], gathered[t][i].at[0, core], ag_s.at[t, i, 0], ag_r.at[t, i, 0], sib)

    def ag_pass(t, i, u):
        part = gathered[t][i].at[u, core]
        return remote(part, part, ag_s.at[t, i, 3 + u], ag_r.at[t, i, 3 + u], sib)

    def ag_self(i):
        return pltpu.make_async_copy(tok.at[:, cols(i)], near[i].at[0, core], loc.at[0, i])

    def refill(i):
        far, own = pl.ds(1, 3), 1 - core
        return (
            pltpu.make_async_copy(hold_dy[i].at[far], near[i].at[far], loc.at[1, i]),
            pltpu.make_async_copy(hold_dy[i].at[0, own], near[i].at[0, own], loc.at[2, i]),
            pltpu.make_async_copy(dy.at[:, cols(i)], near[i].at[0, core], loc.at[3, i]),
        )

    def b0(t, i, e, r):
        k = r - 1
        return remote(send[i].at[e, r, 0], got[t][i].at[e, 0, r], d_s.at[t, i, e, k], d_r.at[t, i, e, k], peer(AXES[i][1], r))

    def b1(t, i, e, r):
        k = r + 2
        return remote(send[i].at[e, r, pl.ds(1, 3)], relay[t][i].at[e, :, r - 1], d_s.at[t, i, e, k], d_r.at[t, i, e, k],
                      peer(AXES[i][1], r))

    def c0(t, i, e, q):
        k = q + 5
        return remote(send[i].at[e, 0, q], got[t][i].at[e, q, 0], d_s.at[t, i, e, k], d_r.at[t, i, e, k], peer(AXES[i][2], q))

    def c1(t, i, e, q):
        k = q + 8
        return remote(relay[t][i].at[e, q - 1], got[t][i].at[e, q, pl.ds(1, 3)], d_s.at[t, i, e, k], d_r.at[t, i, e, k],
                      peer(AXES[i][2], q))

    def rc0(i, e, q):
        k = q - 1
        return remote(send[i].at[e, q, 0], back[i].at[e, 0, q], b_s.at[i, e, k], b_r.at[i, e, k], peer(AXES[i][2], -q))

    def rc1(i, e, q):
        k = q + 2
        return remote(send[i].at[e, q, pl.ds(1, 3)], relay[2][i].at[e, q - 1], b_s.at[i, e, k], b_r.at[i, e, k],
                      peer(AXES[i][2], -q))

    def rb0(i, e, r):
        k = r + 5
        return remote(send[i].at[e, 0, r], back[i].at[e, r, 0], b_s.at[i, e, k], b_r.at[i, e, k], peer(AXES[i][1], -r))

    def rb1(i, e, r):
        k = r + 8
        return remote(relay[2][i].at[e, :, r - 1], back[i].at[e, r, pl.ds(1, 3)], b_s.at[i, e, k], b_r.at[i, e, k],
                      peer(AXES[i][1], -r))

    def z_sib(i, u):
        return remote(near[i].at[u, 1 - core], from_sib[i].at[u], z_s.at[i, u], z_r.at[i, u], sib)

    def z_line(i, u):
        return remote(near[i].at[u, core], last[i].at[u - 1], z_s.at[i, 3 + u], z_r.at[i, 3 + u], peer(AXES[i][0], -u))

    weights = (wg, wu, wd)

    def load_w(n, e):
        return pltpu.make_async_copy(weights[n].at[e], wbuf[n], w_sem.at[n])

    outs = (out_g, out_u, out_d)

    def store_w(n, e):
        return pltpu.make_async_copy(wbuf[n], outs[n].at[e], o_sem.at[n])

    step = (2, 1, 3)

    barrier = pltpu.get_barrier_semaphore()
    for axis in range(3):
        for u in step:
            pl.semaphore_signal(barrier, inc=1, device_id=peer(axis, u), device_id_type=MESH)
    pl.semaphore_signal(barrier, inc=1, device_id=sib, device_id_type=MESH)
    for n in range(3):
        load_w(n, 0).start()
    info[...] = jnp.zeros((32, TOK), F32)
    info[0:TOPK] = ids_in[...].astype(F32)
    info[16:16 + TOPK] = gates_in[...]
    for i in range(3):
        ag_self(i).start()
        ids[i, 0, core] = info[...]
    pl.semaphore_wait(barrier, 10)

    for i in range(3):
        ids_own(i).start()
        for u in step:
            ids_line(i, u).start()

    def gather_start(t):
        for u in (1, 3, 2):
            for i in range(3):
                ag_line(t, i, u).start()
        for i in range(3):
            ag_own(t, i).start()

    def gather_pass(t):
        for u in (1, 3, 2):
            for i in range(3):
                ag_line(t, i, u).wait_recv()
                ag_pass(t, i, u).start()

    def gather_end(t, i):
        ag_own(t, i).wait_recv()
        for u in (1, 2, 3):
            ag_pass(t, i, u).wait_recv()
            ag_pass(t, i, u).wait_send()
            ag_line(t, i, u).wait_send()
        ag_own(t, i).wait_send()

    gather_start(0)
    gather_start(1)
    for i in range(3):
        for u in step:
            ids_line(i, u).wait_recv()
        ids_pass(i).start()

    def build_perm(n, carry):
        row = lax.broadcasted_iota(jnp.int32, (192, TOK), 0) + n * 192
        group = (row * 5462) >> 16
        inner = row - group * 12
        hi, mid, lo = group >> 4, (group >> 2) & 3, group & 3
        rows = pl.ds(pl.multiple_of(n * 192, 192), 192)
        lane = lax.broadcasted_iota(jnp.int32, (192, TOK), 1)
        for way, target in enumerate((lo * 16 + hi * 4 + mid, mid * 16 + lo * 4 + hi)):
            ahead = target * 12 + inner - lane
            for c in range(6):
                perm[way, rows, c * TOK:(c + 1) * TOK] = jnp.where(ahead == c * TOK, 1.0, 0.0).astype(BF)
        return carry

    lax.fori_loop(0, 4, build_perm, 0)
    for i in range(3):
        ids_own(i).wait_recv()
        ids_pass(i).wait_recv()

    before = (lax.broadcasted_iota(jnp.int32, (TOK, TOK), 0) < lax.broadcasted_iota(jnp.int32, (TOK, TOK), 1))
    before = jnp.where(before, 1.0, 0.0).astype(BF)
    line = lax.broadcasted_iota(jnp.int32, (32, TOK), 0)
    for i in range(3):
        ax_a, ax_b, ax_c = AXES[i]
        shift = [0, 0, 0]
        shift[ax_b] = (line >> 2) & 3
        shift[ax_c] = line & 3
        at = [(zyx[n] + shift[n]) & 3 for n in range(3)]
        expert = ((((at[0] * 4 + at[1]) * 4 + at[2]) * 2 + core) * 2 + (line >> 4)).astype(F32)
        for u in range(4):
            for c in range(2):
                s = u * 2 + c
                named = jnp.zeros((32, TOK), F32)
                weight = jnp.zeros((32, TOK), F32)
                for k in range(TOPK):
                    same = ids[i, u, c, k:k + 1, :] == expert
                    named = named + jnp.where(same, 1.0, 0.0)
                    weight = weight + jnp.where(same, ids[i, u, c, 16 + k:17 + k, :], 0.0)
                rank = dot(named.astype(BF), before, NN)
                place = jnp.where(named > 0.5, rank + float(s * CAP), -1.0)
                for e in range(2):
                    key[i, e, :, s * TOK:(s + 1) * TOK] = place[e * 16:(e + 1) * 16]
                    gate[i, e, :, s * TOK:(s + 1) * TOK] = weight[e * 16:(e + 1) * 16]

    slot = lax.broadcasted_iota(jnp.int32, (ROWS, 8 * TOK), 0).astype(F32)

    def build_pick(i, e, weighted, keep=False):
        def one(n, carry):
            same = key[i, e, pl.ds(n, 1), :] == slot
            value = gate[i, e, pl.ds(n, 1), :] if weighted else 1.0
            picked = jnp.where(same, value, 0.0).astype(BF)
            if keep:
                for half in range(2):
                    got[1][i][half, n // 4, lax.rem(n, 4), :, 0:512] = picked[:, half * 512:half * 512 + 512]
            else:
                pick[n] = picked
            return carry

        lax.fori_loop(0, 16, one, 0)

    def dispatch(t, i, e):
        width = PARTS[i][1]
        build_pick(i, e, t == 1)

        def half(h, carry):
            rows = pick[pl.ds(h * 8, 8)].reshape(8 * ROWS, 8 * TOK)
            value = dot(rows, near[i][...].reshape(8 * TOK, width), NN).astype(BF)
            send[i][e, pl.ds(2 * h, 2)] = value.reshape(2, 4, ROWS, width)
            return carry

        lax.fori_loop(0, 2, half, 0)
        got[t][i][e, 0, 0] = send[i][e, 0, 0]
        for r in step:
            b1(t, i, e, r).start()
        for r in step:
            c0(t, i, e, r).start()
        for r in step:
            b0(t, i, e, r).start()

    def forward(t, e):
        for i in range(3):
            for r in step:
                b1(t, i, e, r).wait_recv()
        for q in (1, 3, 2):
            for i in range(3):
                c1(t, i, e, q).start()

    def arrived(t, i, e):
        for r in step:
            b0(t, i, e, r).wait_recv()
            c0(t, i, e, r).wait_recv()
            c1(t, i, e, r).wait_recv()

    def sends_done(t, i, e):
        for r in step:
            b0(t, i, e, r).wait_send()
            b1(t, i, e, r).wait_send()
            c0(t, i, e, r).wait_send()

    def in_order(t, i, e):
        width = PARTS[i][1]

        def half(h, carry):
            rows = pl.ds(pl.multiple_of(h * 384, 384), 384)
            tmp[rows, :] = dot(perm[i - 1, rows, :], got[t][i][e].reshape(16 * ROWS, width), NN).astype(BF)
            return carry

        lax.fori_loop(0, 2, half, 0)
        got[t][i][e] = tmp[...].reshape(4, 4, ROWS, width)

    def each(count, body):
        lax.fori_loop(0, count, lambda n, c: (body(n), c)[1], 0)

    gather_pass(0)
    for i in range(3):
        gather_end(0, i)
        ag_self(i).wait()

    def dispatch_tok(e):
        for i in range(3):
            dispatch(0, i, e)

    each(2, dispatch_tok)
    gather_pass(1)
    each(2, lambda e: forward(0, e))

    for i in range(3):
        gather_end(1, i)
        for one in refill(i):
            one.start()
    for i in range(3):
        for one in refill(i):
            one.wait()

    def dispatch_dy(e):
        for i in range(3):
            sends_done(0, i, e)
            dispatch(1, i, e)

    each(2, dispatch_dy)

    def halves(t, i, e, h):
        return got[t][i][e, pl.ds(2 * h, 2)].reshape(8 * ROWS, PARTS[i][1])

    def first(e):
        for i in range(3):
            arrived(0, i, e)
        for i in (1, 2):
            in_order(0, i, e)
        load_w(0, e).wait()
        load_w(1, e).wait()

        def half(h):
            both = []
            for n in range(2):
                total = dot(halves(0, 0, e, h), wbuf[n][0:768], NN)
                for i in (1, 2):
                    total = total + dot(halves(0, i, e, h), wbuf[n][PARTS[i][0]:PARTS[i][0] + PARTS[i][1]], NN)
                both.append(total)
            pre_gate, pre_up = both
            rows = pl.ds(pl.multiple_of(h * 384, 384), 384)
            sig = jax.nn.sigmoid(pre_gate)
            silu = pre_gate * sig
            act[e, 0, rows] = (silu * pre_up).astype(BF)
            pre[e, 0, rows] = pre_up * sig * (1.0 + pre_gate * (1.0 - sig))
            pre[e, 1, rows] = silu

        each(2, half)
        load_w(0, 1 - e).start()
        load_w(1, 1 - e).start()
        forward(1, e)

    each(2, first)

    def second(e):
        for i in range(3):
            arrived(1, i, e)
        for i in (1, 2):
            in_order(1, i, e)
        for n in range(3):
            load_w(n, e).wait()

        def half(h):
            grad = dot(halves(1, 0, e, h), wbuf[2][:, 0:768], NT)
            for i in (1, 2):
                grad = grad + dot(halves(1, i, e, h), wbuf[2][:, PARTS[i][0]:PARTS[i][0] + PARTS[i][1]], NT)
            rows = pl.ds(pl.multiple_of(h * 384, 384), 384)
            act[e, 1, rows] = (grad * pre[e, 0, rows]).astype(BF)
            act[e, 2, rows] = (grad * pre[e, 1, rows]).astype(BF)

        each(2, half)
        for i in range(3):
            sends_done(1, i, e)
            start, width = PARTS[i]
            if i > 0:
                def turn(h):
                    rows = pl.ds(pl.multiple_of(h * 384, 384), 384)
                    for n in range(2):
                        turned[n, rows] = dot(perm[2 - i, rows, :], act[e, 1 + n], NN).astype(BF)

                each(2, turn)

            def part(h):
                rows = pl.ds(pl.multiple_of(h * 384, 384), 384)
                left = act[e, 1, rows] if i == 0 else turned[0, rows]
                right = act[e, 2, rows] if i == 0 else turned[1, rows]
                total = dot(left, wbuf[0][start:start + width], NT) + dot(right, wbuf[1][start:start + width], NT)
                send[i][e, pl.ds(2 * h, 2)] = total.astype(BF).reshape(2, 4, ROWS, width)

            each(2, part)
            back[i][e, 0, 0] = send[i][e, 0, 0]
            for q in step:
                rc1(i, e, q).start()
            for q in step:
                rb0(i, e, q).start()
            for q in step:
                rc0(i, e, q).start()

        @pl.when(e == 0)
        def _():
            for n in range(3):
                load_w(n, 1).start()

    each(2, second)

    def send_on(e):
        for i in range(3):
            for q in step:
                rc1(i, e, q).wait_recv()
        for r in (1, 3, 2):
            for i in range(3):
                rb1(i, e, r).start()

    def weight_grads(e):
        @pl.when(e == 1)
        def _():
            for n in range(3):
                store_w(n, 0).wait()

        for i in range(3):
            start, width = PARTS[i]
            rows_x = got[0][i][e].reshape(16 * ROWS, width)
            rows_dy = got[1][i][e].reshape(16 * ROWS, width)
            wbuf[0][start:start + width] = dot(rows_x, act[e, 1], TN).astype(BF)
            wbuf[1][start:start + width] = dot(rows_x, act[e, 2], TN).astype(BF)
            wbuf[2][:, start:start + width] = dot(act[e, 0], rows_dy, TN).astype(BF)
        for n in range(3):
            store_w(n, e).start()

    def returned(i, e):
        for r in step:
            rb0(i, e, r).wait_recv()
            rc0(i, e, r).wait_recv()
            rb1(i, e, r).wait_recv()

    def collect(i):
        width = PARTS[i][1]
        build_pick(i, 0, False)
        returned(i, 0)
        for u in range(4):
            rows = pick[:, :, u * 256:(u + 1) * 256].reshape(16 * ROWS, 256)
            total = dot(rows, back[i][0].reshape(16 * ROWS, width), TN).reshape(2, TOK, width)
            near[i][u] = total.astype(BF)

    def collect_last(i, u):
        width = PARTS[i][1]
        lanes = (u % 2) * 256
        rows = got[1][i][u // 2, :, :, :, lanes:lanes + 256].reshape(16 * ROWS, 256)
        total = dot(rows, back[i][1].reshape(16 * ROWS, width), TN).reshape(2, TOK, width)
        near[i][u] = (total + near[i][u].astype(F32)).astype(BF)
        z_sib(i, u).start()

    def both(i, u):
        z_sib(i, u).wait_recv()
        return near[i][u, core].astype(F32) + from_sib[i][u].astype(F32)

    def line_out(i, u):
        near[i][u, core] = both(i, u).astype(BF)
        z_line(i, u).start()

    def tail(e):
        send_on(e)
        weight_grads(e)

    each(2, tail)
    for i in range(3):
        collect(i)
    for i in range(3):
        build_pick(i, 1, False, True)
    for i in range(3):
        returned(i, 1)
        collect_last(i, 2)
    for n, u in enumerate((1, 3, 0)):
        for i in range(3):
            collect_last(i, u)
        for i in range(3):
            line_out(i, (2, 1, 3)[n])
    for i in range(3):
        total = both(i, 0)
        for u in step:
            z_line(i, u).wait_recv()
            total = total + last[i][u - 1].astype(F32)
        out_t[:, PARTS[i][0]:PARTS[i][0] + PARTS[i][1]] = total.astype(BF)

    for n in range(3):
        store_w(n, 1).wait()
    for i in range(3):
        for u in range(4):
            z_sib(i, u).wait_send()
        for u in step:
            z_line(i, u).wait_send()
            ids_line(i, u).wait_send()
        ids_own(i).wait_send()
        ids_pass(i).wait_send()

    def drain(e):
        for i in range(3):
            for r in step:
                c1(0, i, e, r).wait_send()
                c1(1, i, e, r).wait_send()
                rc0(i, e, r).wait_send()
                rc1(i, e, r).wait_send()
                rb0(i, e, r).wait_send()
                rb1(i, e, r).wait_send()

    each(2, drain)


def copy_kernel(*refs):
    src, dst, held, sems = refs[:4], refs[4:8], refs[8:12], refs[12]
    moves = [(0, (pl.ds(0, TOK),))]
    for k in range(4):
        for n in (1, 2, 3):
            size = src[n].shape[1] // 2
            moves.append((n, (k // 2, pl.ds((k % 2) * size, size))))
    into = [pltpu.make_async_copy(src[n].at[at], held[n].at[at], sems.at[0, j]) for j, (n, at) in enumerate(moves)]
    out = [pltpu.make_async_copy(held[n].at[at], dst[n].at[at], sems.at[1, j]) for j, (n, at) in enumerate(moves)]
    for one in into:
        one.start()
    for one, other in zip(into, out):
        one.wait()
        other.start()
    for one in out:
        one.wait()


def hand_over(*arrays):
    any_ = pl.BlockSpec(memory_space=pl.ANY)
    return pl.pallas_call(
        copy_kernel,
        out_shape=[jax.ShapeDtypeStruct(a.shape, a.dtype) for a in arrays],
        in_specs=[any_] * 4,
        out_specs=[any_] * 4,
        scratch_shapes=[pltpu.VMEM(a.shape, a.dtype) for a in arrays] + [pltpu.SemaphoreType.DMA((2, 25))],
        compiler_params=pltpu.CompilerParams(vmem_limit_bytes=63 * 10**6),
        cost_estimate=pl.CostEstimate(flops=0, bytes_accessed=26 * 10**6, transcendentals=0),
    )(*arrays)


def per_device(tokens, out_grad, expert_ids, gate_vals, w_gate, w_up, w_down):
    width = tokens.shape[1]
    any_ = pl.BlockSpec(memory_space=pl.ANY)
    vmem = pl.BlockSpec(memory_space=pltpu.VMEM)
    widths = [p[1] for p in PARTS]
    hbm_shapes = [jax.ShapeDtypeStruct((4, 2, TOK, c), BF) for c in widths]
    for _ in range(3):
        hbm_shapes += [jax.ShapeDtypeStruct((2, 3, 3, ROWS, c), BF) for c in widths]
    scratch = [pltpu.VMEM((4, 2, TOK, c), BF) for c in widths]
    for _ in range(4):
        scratch += [pltpu.VMEM((2, 4, 4, ROWS, c), BF) for c in widths]
    scratch += [pltpu.VMEM((4, TOK, c), BF) for c in widths]
    scratch += [pltpu.VMEM((3, TOK, c), BF) for c in widths]
    dma = pltpu.SemaphoreType.DMA
    scratch += [
        pltpu.VMEM((32, TOK), F32),
        pltpu.VMEM((3, 4, 2, 32, TOK), F32),
        pltpu.VMEM((3, 2, 16, 8 * TOK), F32),
        pltpu.VMEM((3, 2, 16, 8 * TOK), F32),
        pltpu.VMEM((16, ROWS, 8 * TOK), BF),
        pltpu.VMEM((2, 16 * ROWS, 16 * ROWS), BF),
        pltpu.VMEM((16 * ROWS, 640), BF),
        pltpu.VMEM((2, 3, 16 * ROWS, HID), BF),
        pltpu.VMEM((2, 2, 16 * ROWS, HID), F32),
        pltpu.VMEM((2, 16 * ROWS, HID), BF),
        (pltpu.VMEM((width, HID), BF), pltpu.VMEM((width, HID), BF), pltpu.VMEM((HID, width), BF)),
        dma((4, 3)),
        dma((3, 5)), dma((3, 5)),
        dma((2, 3, 7)), dma((2, 3, 7)),
        dma((2, 3, 2, 12)), dma((2, 3, 2, 12)),
        dma((3, 2, 12)), dma((3, 2, 12)),
        dma((3, 7)), dma((3, 7)),
        dma((3,)), dma((3,)),
    ]
    results = pl.pallas_call(
        kernel,
        out_shape=[
            jax.ShapeDtypeStruct(tokens.shape, BF),
            jax.ShapeDtypeStruct(w_gate.shape, BF),
            jax.ShapeDtypeStruct(w_up.shape, BF),
            jax.ShapeDtypeStruct(w_down.shape, BF),
        ] + hbm_shapes,
        in_specs=[vmem, vmem] + [any_] * 5,
        out_specs=[vmem] + [any_] * (3 + len(hbm_shapes)),
        scratch_shapes=scratch,
        compiler_params=pltpu.CompilerParams(collective_id=0, has_side_effects=True, vmem_limit_bytes=63 * 10**6),
        cost_estimate=pl.CostEstimate(flops=60 * 10**9, bytes_accessed=60 * 10**6, transcendentals=10**6),
    )(expert_ids.T, gate_vals.T, tokens, out_grad, w_gate, w_up, w_down)
    return hand_over(*results[:4])


def solution(mesh):
    rows = P(("group", "member"), None)
    whole = P(("group", "member"), None, None)
    return jax.shard_map(
        per_device,
        mesh=mesh,
        in_specs=(rows, rows, rows, rows, whole, whole, whole),
        out_specs=(rows, whole, whole, whole),
        check_vma=False,
    )
```
